512 devices in a mesh: dp: 32 (over z_hi, y, core), tensor: 16 (over z_lo, x).
Axes of the slice: x: 4, y: 4, z: 16 (z_hi: 4, z_lo: 4; z = z_hi * 4 + z_lo), core: 2. Of those that a mesh axis runs over, the one named last changes fastest.
Arguments:
- attention: bfloat16 [8192, 4096], P('dp', 'tensor'), may hold values from -6 to 6
- residual: bfloat16 [8192, 4096], P(('dp', 'tensor'))
- out_weight: bfloat16 [4096, 4096], P('tensor'), may hold values from -0.09375 to 0.09375
- norm_gain: float32 [4096], replicated, may hold values from 0.1 to 1.9
- grad_normed: bfloat16 [8192, 4096], P(('dp', 'tensor'))
- grad_resid: bfloat16 [8192, 4096], P(('dp', 'tensor')), may hold values from -6 to 6
Outputs:
- normed: bfloat16 [8192, 4096], P(('dp', 'tensor'))
- stream_out: bfloat16 [8192, 4096], P(('dp', 'tensor'))
- stream_grad: bfloat16 [8192, 4096], P(('dp', 'tensor'))
- attn_grad: bfloat16 [8192, 4096], P('dp', 'tensor')
- weight_grad: float32 [4096, 4096], P('tensor', 'dp')
- gain_grad: float32 [4096], replicated
The draws below stay inside these ranges and needn't reach their ends.
All inputs are finite; a program needn't handle non-finite values.
Results may differ from the reference program's by a relative error of at most 0.02.
Values may be sent and summed in bfloat16 or wider, within the bound.
No kernel may reach another device: no remote copies, remote signals or barrier semaphores. Data moves between devices by JAX's collectives and lax.ppermute only.
A program may use at most 64 MiB of HBM per device.

```python
import math
import jax
import jax.numpy as jnp
from jax import lax

D = 4096
HEADS = 32
HEAD = 128
TOK_DP = 256
HD_ALL = 4096
TOKENS = 8192
N_DP = 32
N_TENSOR = 16


def draw_residual(key, part):
    key = jax.random.fold_in(key, 11)
    row_key, col_key, base_key = jax.random.split(key, 3)
    base = jax.random.normal(base_key, (TOKENS, D), jnp.float32)
    row_scale = jnp.exp(jax.random.uniform(row_key, (TOKENS, 1), jnp.float32, math.log(0.3), math.log(3.0)))
    col_scale = jnp.exp(jax.random.uniform(col_key, (1, D), jnp.float32, math.log(0.5), math.log(2.0)))
    return jnp.clip(base * row_scale * col_scale, -30.0, 30.0).astype(jnp.bfloat16)


def draw_grad_normed(key, part):
    key = jax.random.fold_in(key, 23)
    base_key = jax.random.fold_in(key, 0)
    ramp = 0.5 + 1.5 * jnp.arange(TOKENS, dtype=jnp.float32)[:, None] / max(TOKENS - 1, 1)
    base = jax.random.normal(base_key, (TOKENS, D), jnp.float32)
    return jnp.clip(base * ramp, -12.0, 12.0).astype(jnp.bfloat16)


def level_of(rng, extent, shards, least, top_value):
    gain, own = 1.0, jax.random.fold_in(rng, 6)
    for position, blocks in shards:
        heights = jnp.exp(jax.random.uniform(jax.random.fold_in(own, position), (blocks,), jnp.float32, least / len(shards), top_value / len(shards)))
        gain = gain * jnp.repeat(heights, extent[position] // blocks).reshape([-1 if axis == position else 1 for axis in range(len(extent))])
    return gain


def scatter_about(stream_key, extent, spread, reach, shards=(), held_as=jnp.bfloat16):
    values = spread * jax.random.normal(stream_key, extent, jnp.float32)
    if shards:
        values = values * level_of(stream_key, extent, shards, -0.22, 0.18)
    return jnp.clip(values, -reach, reach).astype(held_as)


def setup_inputs(seed: int = 0) -> dict:
    key_list = jax.random.split(jax.random.key(seed), 7)
    return {
        "attention": scatter_about(key_list[0], (TOKENS, HD_ALL), 1.0, 6.0, ((0, 32), (1, 16))),
        "residual": draw_residual(jax.random.fold_in(key_list[6], 71), 0),
        "out_weight": scatter_about(key_list[2], (HD_ALL, D), HD_ALL ** -0.5, 0.09375, ((0, 16),)),
        "norm_gain": jnp.clip(1.0 + 0.18 * jax.random.normal(key_list[3], (D,), jnp.float32), 0.1, 1.9),
        "grad_normed": draw_grad_normed(jax.random.fold_in(key_list[6], 71), 0),
        "grad_resid": scatter_about(key_list[5], (TOKENS, D), 1.0, 6.0, ((0, 512),)),
    }


def reference(attention, residual, out_weight, norm_gain, grad_normed, grad_resid):
    head_cols = HEADS * HEAD // N_TENSOR
    row_total = attention.shape[0]
    attn_pieces = attention.reshape(row_total, N_TENSOR, head_cols).transpose(1, 0, 2)
    weight_pieces = out_weight.reshape(N_TENSOR, head_cols, D)

    def add_piece(running, couple):
        piece = jnp.dot(couple[0], couple[1], preferred_element_type=jnp.float32).astype(jnp.bfloat16)
        piece = lax.optimization_barrier(piece)
        return (running + piece.astype(jnp.float32), None)
    projected, _ = lax.scan(add_piece, jnp.zeros((row_total, D), jnp.float32), (attn_pieces, weight_pieces))
    stream_out = (residual.astype(jnp.float32) + projected).astype(jnp.bfloat16)
    values = stream_out.astype(jnp.float32)
    inv_rms = lax.rsqrt(lax.optimization_barrier(jnp.mean(values * values, axis=-1, keepdims=True)) + 1e-05)
    unit_rows = values * inv_rms
    normed = (unit_rows * norm_gain).astype(jnp.bfloat16)
    upstream = grad_normed.astype(jnp.float32)
    gain_grad = lax.optimization_barrier(jnp.sum(upstream * unit_rows, axis=0))
    scaled_grad = upstream * norm_gain
    inner = lax.optimization_barrier(jnp.mean(scaled_grad * unit_rows, axis=-1, keepdims=True))
    stream_grad = (grad_resid.astype(jnp.float32) + inv_rms * (scaled_grad - unit_rows * inner)).astype(jnp.bfloat16)
    attn_grad = lax.dot_general(stream_grad, out_weight, (((1,), (1,)), ((), ())), preferred_element_type=jnp.float32).astype(jnp.bfloat16)
    attn_blocks = attention.reshape(N_DP, TOK_DP, HEADS * HEAD)
    grad_blocks = stream_grad.reshape(N_DP, TOK_DP, D)

    def add_block(running, couple):
        piece = lax.dot_general(couple[0], couple[1], (((0,), (0,)), ((), ())), preferred_element_type=jnp.float32).astype(jnp.bfloat16)
        piece = lax.optimization_barrier(piece)
        return (running + piece.astype(jnp.float32), None)
    weight_grad, _ = lax.scan(add_block, jnp.zeros((HEADS * HEAD, D), jnp.float32), (attn_blocks, grad_blocks))
    return (normed, stream_out, stream_grad, attn_grad, weight_grad, gain_grad)
```

```python
import jax
import jax.numpy as jnp
from jax import lax
from jax.experimental import pallas as pl
from jax.experimental.pallas import tpu as pltpu
from jax.sharding import Mesh, PartitionSpec as P

BF16, F32 = jnp.bfloat16, jnp.float32
AXES = ("zh", "y", "c", "zl", "x")
PARAMS = pltpu.CompilerParams(vmem_limit_bytes=48 * 2**20)
SCALAR = pl.BlockSpec(memory_space=pltpu.SMEM)
WHOLE = pl.BlockSpec(memory_space=pltpu.VMEM)


def shape(dims, dtype=BF16):
    return jax.ShapeDtypeStruct(dims, dtype)


def call(kernel, out_shape, *args):
    specs = [SCALAR if a.dtype == jnp.int32 else WHOLE for a in args]
    return pl.pallas_call(kernel, out_shape=out_shape, in_specs=specs, compiler_params=PARAMS)(*args)


def a2a(value, axes):
    return lax.all_to_all(value, axes, 0, 0, tiled=True)


def ring(step):
    return [(i, (i + step) % 4) for i in range(4)]


def forward_kernel(yc_ref, att_ref, weight_ref, out_ref, cols_ref):
    att = jnp.concatenate(
        [att_ref[z * 64 + x * 16 : z * 64 + x * 16 + 16] for x in range(4) for z in range(4)]
    )
    out_ref[...] = jnp.dot(att, weight_ref[...], preferred_element_type=F32).astype(BF16)
    for h in range(4):
        start = pl.multiple_of(yc_ref[0] * 128 + h * 1024, 128)
        cols_ref[:, h * 128 : h * 128 + 128] = weight_ref[:, pl.ds(start, 128)]


def norm_kernel(
    parts_ref, residual_ref, gain_ref, upstream_ref, resid_grad_ref,
    normed_ref, stream_ref, grad_ref, cols_ref, gain_grad_ref,
):
    projected = parts_ref[0].astype(F32)
    for k in range(1, 4):
        projected += parts_ref[k].astype(F32)
    stream_out = (residual_ref[...].astype(F32) + projected).astype(BF16)
    stream_ref[...] = stream_out
    values = stream_out.astype(F32)
    inv_rms = lax.rsqrt(jnp.mean(values * values, axis=-1, keepdims=True) + 1e-05)
    unit_rows = values * inv_rms
    gain = gain_ref[...]
    normed_ref[...] = (unit_rows * gain).astype(BF16)
    upstream = upstream_ref[...].astype(F32)
    gain_grad = jnp.sum(upstream * unit_rows, axis=0, keepdims=True)
    scaled = upstream * gain
    inner = jnp.mean(scaled * unit_rows, axis=-1, keepdims=True)
    grad = (resid_grad_ref[...].astype(F32) + inv_rms * (scaled - unit_rows * inner)).astype(BF16)
    grad_ref[...] = grad
    for c in range(2):
        for y in range(4):
            for h in range(4):
                start = (h * 8 + y * 2 + c) * 128
                for z in range(4):
                    to = (c * 4 + y) * 4 + z
                    cols_ref[to, :, h * 128 : h * 128 + 128] = grad[:, start : start + 128]
                    gain_grad_ref[to, :, h * 128 : h * 128 + 128] = gain_grad[:, start : start + 128]


def weight_kernel(at_ref, gain_ref, att_ref, *refs):
    x, zh = at_ref[0], at_ref[1]
    total = jnp.zeros((256, 512), F32)
    for piece_ref, step in zip(refs[:4], (0, 3, 1, 2)):
        att = att_ref[:, :, lax.rem(x + step, 4)].reshape(512, 256)
        total += lax.dot_general(
            att, piece_ref[...], (((0,), (0,)), ((), ())), preferred_element_type=F32
        )
    refs[8][...] = total
    gain = gain_ref[...]
    upper = gain.astype(BF16)
    lower = (gain - upper.astype(F32)).astype(BF16)
    for j in range(4):
        start = pl.multiple_of(lax.rem(zh + j, 4) * 128, 128)
        refs[4 + j][:256] = refs[8][:, pl.ds(start, 128)].astype(BF16)
        refs[4 + j][256:288] = upper
        refs[4 + j][288:] = lower


def weight_sum_kernel(*refs):
    total = refs[0][...].astype(F32)
    for ref in refs[1:4]:
        total += ref[...].astype(F32)
    refs[4][...] = total[:256]
    refs[5][...] = total[256:288] + total[288:]


def back_kernel(at_ref, weight_ref, *refs):
    for piece_ref, step in zip(refs[:4], (0, 3, 1, 2)):
        rows = lax.dot_general(
            piece_ref[...], weight_ref[...], (((1,), (1,)), ((), ())), preferred_element_type=F32
        )
        refs[4][:, :, lax.rem(at_ref[0] + step, 4)] = rows.reshape(8, 4, 16, 256).astype(BF16)


def local(attention, residual, out_weight, norm_gain, grad_normed, grad_resid):
    zh, x, y, c = (lax.axis_index(n).astype(jnp.int32) for n in ("zh", "x", "y", "c"))
    at = jnp.stack([x, zh, c])

    partial, weight_cols = call(
        forward_kernel,
        (shape((256, 4096)), shape((256, 512))),
        (y * 2 + c).reshape(1),
        attention,
        out_weight,
    )
    att_all = lax.all_gather(attention, ("c", "y"), axis=0, tiled=True)
    by_x = a2a(partial, "x").reshape(4, 64, 4096)
    sum_x = jnp.sum(by_x.astype(F32), axis=0).astype(BF16)
    by_z = a2a(sum_x, "zl").reshape(4, 16, 4096)
    by_z, att_all = lax.optimization_barrier((by_z, att_all))

    normed, stream_out, stream_grad, cols, gain = call(
        norm_kernel,
        (shape((16, 4096)),) * 3 + (shape((32, 16, 512)), shape((32, 1, 512), F32)),
        by_z,
        residual,
        norm_gain.reshape(1, 4096),
        grad_normed,
        grad_resid,
    )

    grads = a2a(cols, ("c", "y", "zl")).reshape(512, 512)
    grads, gain = lax.optimization_barrier((grads, gain))
    pieces = [grads] + [lax.ppermute(grads, "x", ring(k)) for k in (1, 3, 2)]

    gain = jnp.sum(a2a(gain, ("c", "y", "zl")), axis=0, keepdims=True)
    gain = a2a(jnp.broadcast_to(gain, (32, 1, 512)), ("c", "y", "x"))
    gain = jnp.sum(gain.reshape(8, 4, 4, 128), axis=1).reshape(32, 128)

    blocks = pl.pallas_call(
        weight_kernel,
        out_shape=(shape((320, 128)),) * 4,
        in_specs=[SCALAR] + [WHOLE] * 6,
        scratch_shapes=[pltpu.VMEM((256, 512), F32)],
        compiler_params=PARAMS,
    )(at, gain, att_all.reshape(8, 4, 4, 16, 256), *pieces)
    moved = [lax.ppermute(blocks[k], "zh", ring(k)) for k in (1, 3, 2)]
    weight_grad, gain = call(
        weight_sum_kernel, (shape((256, 128), F32), shape((32, 128), F32)), blocks[0], *moved
    )
    gain_grad = gain.reshape(2, 4, 4, 128).transpose(2, 1, 0, 3).reshape(4096)

    weight_cols, _ = lax.optimization_barrier((weight_cols, blocks[0]))
    back = call(back_kernel, shape((8, 4, 4, 16, 256)), at, weight_cols, *pieces)
    back = back.reshape(8, 256, 256)
    attn_grad = lax.psum_scatter(back, ("c", "y"), scatter_dimension=0, tiled=True).reshape(256, 256)
    return (normed, stream_out, stream_grad, attn_grad, weight_grad, gain_grad)


def solution(mesh):
    fine = Mesh(mesh.devices.reshape(4, 4, 2, 4, 4), AXES)
    dp, tensor = ("zh", "y", "c"), ("zl", "x")
    rows = P(dp + tensor, None)
    return jax.shard_map(
        local,
        mesh=fine,
        in_specs=(P(dp, tensor), rows, P(tensor, None), P(), rows, rows),
        out_specs=(rows, rows, rows, P(dp, tensor), P(tensor, dp), P()),
        check_vma=False,
    )
```

```python
import jax
import jax.numpy as jnp
from jax import lax
from jax.experimental import pallas as pl
from jax.experimental.pallas import tpu as pltpu
from jax.sharding import Mesh, PartitionSpec as P

BF16, F32 = jnp.bfloat16, jnp.float32
AXES = ("zh", "y", "c", "zl", "x")
PARAMS = pltpu.CompilerParams(vmem_limit_bytes=48 * 2**20)
SCALAR = pl.BlockSpec(memory_space=pltpu.SMEM)
WHOLE = pl.BlockSpec(memory_space=pltpu.VMEM)


def shape(dims, dtype=BF16):
    return jax.ShapeDtypeStruct(dims, dtype)


def call(kernel, out_shape, *args):
    specs = [SCALAR if a.dtype == jnp.int32 else WHOLE for a in args]
    return pl.pallas_call(kernel, out_shape=out_shape, in_specs=specs, compiler_params=PARAMS)(*args)


def a2a(value, axes):
    return lax.all_to_all(value, axes, 0, 0, tiled=True)


def ring(step):
    return [(i, (i + step) % 4) for i in range(4)]


def regroup_kernel(att_ref, out_ref):
    for x in range(4):
        for z in range(4):
            rows = att_ref[z * 64 + x * 16 : z * 64 + x * 16 + 16]
            for y in range(4):
                out_ref[y * 4 + x, z * 16 : z * 16 + 16] = rows


def columns_kernel(yc_ref, weight_ref, out_ref, sems):
    copies = [
        pltpu.make_async_copy(
            weight_ref.at[:, pl.ds(pl.multiple_of(yc_ref[0] * 128 + h * 1024, 128), 128)],
            out_ref.at[:, h * 128 : h * 128 + 128],
            sems.at[h],
        )
        for h in range(4)
    ]
    for copy in copies:
        copy.start()
    for copy in copies:
        copy.wait()


def columns(yc, weight):
    return pl.pallas_call(
        columns_kernel,
        out_shape=shape((256, 512)),
        in_specs=[SCALAR, pl.BlockSpec(memory_space=pl.ANY)],
        scratch_shapes=[pltpu.SemaphoreType.DMA((4,))],
    )(yc, weight)


def forward_kernel(c_ref, own_ref, other_ref, *refs):
    c, x = c_ref[0], c_ref[1]
    for att_ref, core in ((own_ref, c), (other_ref, 1 - c)):
        total = jnp.zeros((256, 512), F32)
        for j in range(4):
            att = att_ref[:, lax.rem(x + j, 4)].reshape(256, 256)
            total += jnp.dot(att, refs[j][...], preferred_element_type=F32)
        refs[4][pl.ds(core * 16, 16)] = total.astype(BF16).reshape(16, 16, 512)


def norm_kernel(
    parts_ref, residual_ref, gain_ref, upstream_ref, resid_grad_ref,
    normed_ref, stream_ref, grad_ref, cols_ref, projected_ref,
):
    for c in range(2):
        for y in range(4):
            at = (c * 4 + y) * 4
            total = parts_ref[at].astype(F32)
            for k in range(1, 4):
                total += parts_ref[at + k].astype(F32)
            for h in range(4):
                start = (h * 8 + y * 2 + c) * 128
                projected_ref[:, start : start + 128] = total[:, h * 128 : h * 128 + 128]
    projected = projected_ref[...]
    stream_out = (residual_ref[...].astype(F32) + projected).astype(BF16)
    stream_ref[...] = stream_out
    values = stream_out.astype(F32)
    inv_rms = lax.rsqrt(jnp.mean(values * values, axis=-1, keepdims=True) + 1e-05)
    unit_rows = values * inv_rms
    gain = gain_ref[...]
    normed_ref[...] = (unit_rows * gain).astype(BF16)
    upstream = upstream_ref[...].astype(F32)
    gain_grad = jnp.sum(upstream * unit_rows, axis=0, keepdims=True)
    scaled = upstream * gain
    inner = jnp.mean(scaled * unit_rows, axis=-1, keepdims=True)
    grad = (resid_grad_ref[...].astype(F32) + inv_rms * (scaled - unit_rows * inner)).astype(BF16)
    grad_ref[...] = grad
    for k in range(32):
        rows = jnp.broadcast_to(gain_grad[:, k * 128 : k * 128 + 128], (32, 128))
        cols_ref[:, 64 + k : 65 + k] = rows.astype(BF16)[:, None]
    for c in range(2):
        for y in range(4):
            for h in range(4):
                start = (h * 8 + y * 2 + c) * 128
                for z in range(4):
                    to = (c * 4 + y) * 4 + z
                    cols_ref[to, h * 16 : h * 16 + 16] = grad[:, start : start + 128]


def unpack_kernel(parts_ref, grads_ref, gain_ref):
    gain_ref[...] = jnp.sum(parts_ref[:, 64:].astype(F32), axis=0)
    for h in range(4):
        grads_ref[:, h * 128 : h * 128 + 128] = parts_ref[:, h * 16 : h * 16 + 16].reshape(512, 128)


def weight_kernel(at_ref, own_ref, other_ref, grads_ref, gain_ref, out_ref):
    c = at_ref[0]
    gain = gain_ref[...]
    upper = gain.astype(BF16)
    lower = (gain - upper.astype(F32)).astype(BF16)
    for x in range(4):
        total = jnp.zeros((256, 512), F32)
        for att_ref, core in ((own_ref, c), (other_ref, 1 - c)):
            total += lax.dot_general(
                att_ref[:, x].reshape(256, 256),
                grads_ref[pl.ds(pl.multiple_of(core * 256, 256), 256)],
                (((0,), (0,)), ((), ())),
                preferred_element_type=F32,
            )
        total = total.astype(BF16)
        for h in range(4):
            out_ref[x, h * 256 : h * 256 + 256] = total[:, h * 128 : h * 128 + 128]
        out_ref[x, 1024:1056] = upper
        out_ref[x, 1056:] = lower


def weight_x_kernel(parts_ref, out_ref):
    total = parts_ref[0].astype(F32)
    for k in range(1, 4):
        total += parts_ref[k].astype(F32)
    for h in range(4):
        out_ref[h, :256] = total[h * 256 : h * 256 + 256].astype(BF16)
        out_ref[h, 256:] = (total[1024:1056] + total[1056:]).astype(BF16)


def weight_zh_kernel(parts_ref, weight_ref, gain_ref):
    total = parts_ref[0].astype(F32)
    for k in range(1, 4):
        total += parts_ref[k].astype(F32)
    weight_ref[...] = total[:256]
    gain_ref[...] = total[256:]


def back_kernel(at_ref, grads_ref, *refs):
    for out_ref, core in ((refs[4], 1 - at_ref[0]), (refs[5], at_ref[0])):
        rows = grads_ref[pl.ds(pl.multiple_of(core * 256, 256), 256)]
        for j in range(4):
            back = lax.dot_general(
                rows, refs[j][...], (((1,), (1,)), ((), ())), preferred_element_type=F32
            )
            back = back.reshape(4, 64, 256).astype(out_ref.dtype)
            for y in range(4):
                out_ref[lax.rem(y + 4 - at_ref[2], 4), j] = back[y]


def add_core_kernel(keep_ref, other_ref, *refs):
    for j in range(4):
        refs[j][...] = (keep_ref[j] + other_ref[j].astype(F32)).astype(BF16)


def add_y_kernel(*refs):
    total = refs[0][...].astype(F32)
    for ref in refs[1:4]:
        total += ref[...].astype(F32)
    for j in range(4):
        refs[4 + j][...] = total[j].astype(BF16)


def join_kernel(at_ref, *refs):
    for ref, step in zip(refs[:4], (0, 3, 1, 2)):
        refs[4][:, lax.rem(at_ref[1] + step, 4)] = ref[...].reshape(4, 16, 256)


def local(attention, residual, out_weight, norm_gain, grad_normed, grad_resid):
    x, y, c = (lax.axis_index(n).astype(jnp.int32) for n in ("x", "y", "c"))
    at = jnp.stack([c, x, y])
    swap = [(0, 1), (1, 0)]

    weight = columns((y * 2 + c).reshape(1), out_weight)
    weights = [weight] + [lax.ppermute(weight, "x", ring(4 - j)) for j in (1, 2, 3)]

    own = call(regroup_kernel, shape((16, 64, 256)), attention)
    own = a2a(own, ("y", "x")).reshape(4, 4, 64, 256)
    own, *weights = lax.optimization_barrier((own, *weights))
    other = lax.ppermute(own, "c", swap)

    parts = call(forward_kernel, shape((32, 16, 512)), at, own, other, *weights)
    parts = a2a(parts, ("c", "y", "zl"))

    normed, stream_out, stream_grad, cols = pl.pallas_call(
        norm_kernel,
        out_shape=(shape((16, 4096)),) * 3 + (shape((32, 96, 128)),),
        in_specs=[WHOLE] * 5,
        scratch_shapes=[pltpu.VMEM((16, 4096), F32)],
        compiler_params=PARAMS,
    )(parts, residual, norm_gain.reshape(1, 4096), grad_normed, grad_resid)

    grads, gain = call(
        unpack_kernel, (shape((512, 512)), shape((32, 128), F32)), a2a(cols, ("c", "y", "zl"))
    )

    blocks = call(weight_kernel, shape((4, 1088, 128)), at, own, other, grads, gain)
    blocks, weights[0] = lax.optimization_barrier((blocks, weights[0]))
    by_zh = call(weight_x_kernel, shape((4, 288, 128)), a2a(blocks, "x"))

    send, keep = call(
        back_kernel,
        (shape((4, 4, 64, 256)), shape((4, 4, 64, 256), F32)),
        at,
        grads,
        *weights,
    )
    back = call(add_core_kernel, (shape((4, 64, 256)),) * 4, keep, lax.ppermute(send, "c", swap))
    moved = [lax.ppermute(back[k], "y", ring(k)) for k in (1, 3, 2)]
    by_zh, moved[0] = lax.optimization_barrier((by_zh, moved[0]))
    parts = a2a(by_zh, "zh")
    back = call(add_y_kernel, (shape((64, 256)),) * 4, back[0], *moved)
    moved = [lax.ppermute(back[k], "x", ring(k)) for k in (1, 3, 2)]
    parts, moved[2] = lax.optimization_barrier((parts, moved[2]))
    weight_grad, gain = call(
        weight_zh_kernel, (shape((256, 128), F32), shape((32, 128), F32)), parts
    )
    attn_grad = call(join_kernel, shape((4, 4, 16, 256)), at, back[0], *moved).reshape(256, 256)
    return (normed, stream_out, stream_grad, attn_grad, weight_grad, gain.reshape(4096))


def solution(mesh):
    fine = Mesh(mesh.devices.reshape(4, 4, 2, 4, 4), AXES)
    dp, tensor = ("zh", "y", "c"), ("zl", "x")
    rows = P(dp + tensor, None)
    return jax.shard_map(
        local,
        mesh=fine,
        in_specs=(P(dp, tensor), rows, P(tensor, None), P(), rows, rows),
        out_specs=(rows, rows, rows, P(dp, tensor), P(tensor, dp), P()),
        check_vma=False,
    )
```

```python
import jax
import jax.numpy as jnp
from jax import lax
from jax.experimental import pallas as pl
from jax.experimental.pallas import tpu as pltpu
from jax.sharding import Mesh, PartitionSpec as P

BF16, F32 = jnp.bfloat16, jnp.float32
AXES = ("zh", "y", "c", "zl", "x")
PARAMS = pltpu.CompilerParams(vmem_limit_bytes=48 * 2**20)
SCALAR = pl.BlockSpec(memory_space=pltpu.SMEM)
WHOLE = pl.BlockSpec(memory_space=pltpu.VMEM)


def shape(dims, dtype=BF16):
    return jax.ShapeDtypeStruct(dims, dtype)


def call(kernel, out_shape, *args):
    specs = [SCALAR if a.dtype == jnp.int32 else WHOLE for a in args]
    return pl.pallas_call(kernel, out_shape=out_shape, in_specs=specs, compiler_params=PARAMS)(*args)


def a2a(value, axes):
    return lax.all_to_all(value, axes, 0, 0, tiled=True)


def ring(step):
    return [(i, (i + step) % 4) for i in range(4)]


def pieces_kernel(at_ref, att_hbm_ref, weight_ref, out_ref, att_ref, quarter, sems):
    first = pltpu.make_async_copy(att_hbm_ref, att_ref, sems.at[0])
    copy = pltpu.make_async_copy(
        weight_ref.at[pl.ds(pl.multiple_of(at_ref[2] * 64, 64), 64)], quarter, sems.at[1]
    )
    first.start()
    copy.start()
    first.wait()
    for x in range(4):
        for z in range(4):
            rows = att_ref[z * 64 + x * 16 : z * 64 + x * 16 + 16]
            for y in range(4):
                out_ref[y * 4 + x, z * 16 : z * 16 + 16] = rows
    copy.wait()
    for y in range(4):
        for h in range(4):
            start = pl.multiple_of((h * 8 + y * 2 + at_ref[0]) * 128, 128)
            piece = quarter[:, pl.ds(start, 128)]
            rows, cols = 64 + h // 2 * 64, h % 2 * 128
            for x in range(4):
                out_ref[y * 4 + x, rows : rows + 64, cols : cols + 128] = piece


def pieces(at, attention, weight):
    return pl.pallas_call(
        pieces_kernel,
        out_shape=shape((16, 192, 256)),
        in_specs=[SCALAR] + [pl.BlockSpec(memory_space=pl.ANY)] * 2,
        scratch_shapes=[
            pltpu.VMEM((256, 256), BF16),
            pltpu.VMEM((64, 4096), BF16),
            pltpu.SemaphoreType.DMA((2,)),
        ],
    )(at, attention, weight)


def split_kernel(parts_ref, att_ref, weight_ref):
    att_ref[...] = parts_ref[:, :, :64]
    for x in range(4):
        for half in range(2):
            weight_ref[x * 256 : x * 256 + 256, half * 256 : half * 256 + 256] = parts_ref[
                :, x, 64 + half * 64 : 128 + half * 64
            ].reshape(256, 256)


def apart(bits):
    return [(i, i ^ bits) for i in range(4)]


def forward_kernel(c_ref, own_ref, other_ref, weight_ref, out_ref):
    c = c_ref[0]
    for att_ref, core in ((own_ref, c), (other_ref, 1 - c)):
        total = jnp.zeros((256, 512), F32)
        for x in range(4):
            total += jnp.dot(
                att_ref[:, x].reshape(256, 256),
                weight_ref[x * 256 : x * 256 + 256],
                preferred_element_type=F32,
            )
        total = total.astype(BF16)
        for y in range(4):
            for z in range(4):
                at = (y * 4 + z) * 16
                out_ref[z * 8 + core * 4 + y] = total[at : at + 16]


def norm_kernel(
    parts_ref, residual_ref, gain_ref, upstream_ref, resid_grad_ref,
    normed_ref, stream_ref, grad_ref, cols_ref, projected_ref,
):
    for c in range(2):
        for y in range(4):
            at = c * 4 + y
            total = parts_ref[at].astype(F32)
            for k in range(1, 4):
                total += parts_ref[at + k * 8].astype(F32)
            for h in range(4):
                start = (h * 8 + y * 2 + c) * 128
                projected_ref[:, start : start + 128] = total[:, h * 128 : h * 128 + 128]
    projected = projected_ref[...]
    stream_out = (residual_ref[...].astype(F32) + projected).astype(BF16)
    stream_ref[...] = stream_out
    values = stream_out.astype(F32)
    inv_rms = lax.rsqrt(jnp.mean(values * values, axis=-1, keepdims=True) + 1e-05)
    unit_rows = values * inv_rms
    gain = gain_ref[...]
    normed_ref[...] = (unit_rows * gain).astype(BF16)
    upstream = upstream_ref[...].astype(F32)
    gain_grad = jnp.sum(upstream * unit_rows, axis=0, keepdims=True)
    scaled = upstream * gain
    inner = jnp.mean(scaled * unit_rows, axis=-1, keepdims=True)
    grad = (resid_grad_ref[...].astype(F32) + inv_rms * (scaled - unit_rows * inner)).astype(BF16)
    grad_ref[...] = grad
    for k in range(32):
        rows = jnp.broadcast_to(gain_grad[:, k * 128 : k * 128 + 128], (32, 128))
        cols_ref[:, 64 + k : 65 + k] = rows.astype(BF16)[:, None]
    for c in range(2):
        for y in range(4):
            for h in range(4):
                start = (h * 8 + y * 2 + c) * 128
                for z in range(4):
                    to = (z * 2 + c) * 4 + y
                    cols_ref[to, h * 16 : h * 16 + 16] = grad[:, start : start + 128]


def unpack_kernel(parts_ref, grads_ref, gain_ref):
    gain_ref[...] = jnp.sum(parts_ref[:, 64:].astype(F32), axis=0)
    for k in range(32):
        at = (k % 8 * 4 + k // 8) * 16
        for h in range(4):
            grads_ref[at : at + 16, h * 128 : h * 128 + 128] = parts_ref[k, h * 16 : h * 16 + 16]


def weight_kernel(at_ref, own_ref, other_ref, grads_ref, gain_ref, out_ref):
    c = at_ref[0]
    gain = gain_ref[...]
    upper = gain.astype(BF16)
    lower = (gain - upper.astype(F32)).astype(BF16)
    for x in range(4):
        total = jnp.zeros((256, 512), F32)
        for att_ref, core in ((own_ref, c), (other_ref, 1 - c)):
            total += lax.dot_general(
                att_ref[:, x].reshape(256, 256),
                grads_ref[pl.ds(pl.multiple_of(core * 256, 256), 256)],
                (((0,), (0,)), ((), ())),
                preferred_element_type=F32,
            )
        total = total.astype(BF16)
        for h in range(4):
            out_ref[x, h * 256 : h * 256 + 256] = total[:, h * 128 : h * 128 + 128]
        out_ref[x, 1024:1056] = upper
        out_ref[x, 1056:] = lower


def weight_x_kernel(parts_ref, out_ref):
    total = parts_ref[0].astype(F32)
    for k in range(1, 4):
        total += parts_ref[k].astype(F32)
    for h in range(4):
        out_ref[h, :256] = total[h * 256 : h * 256 + 256].astype(BF16)
        out_ref[h, 256:] = (total[1024:1056] + total[1056:]).astype(BF16)


def weight_zh_kernel(parts_ref, weight_ref, gain_ref):
    total = parts_ref[0].astype(F32)
    for k in range(1, 4):
        total += parts_ref[k].astype(F32)
    weight_ref[...] = total[:256]
    gain_ref[...] = total[256:]


def place(there, here):
    apart = there ^ here
    return (apart & 1) * 2 + (apart >> 1)


def back_kernel(at_ref, grads_ref, weight_ref, send_ref, keep_ref):
    for out_ref, core in ((send_ref, 1 - at_ref[0]), (keep_ref, at_ref[0])):
        rows = grads_ref[pl.ds(pl.multiple_of(core * 256, 256), 256)]
        for j in range(4):
            start = pl.multiple_of(lax.rem(at_ref[1] + j, 4) * 256, 256)
            back = lax.dot_general(
                rows,
                weight_ref[pl.ds(start, 256)],
                (((1,), (1,)), ((), ())),
                preferred_element_type=F32,
            )
            back = back.reshape(4, 64, 256).astype(out_ref.dtype)
            for y in range(4):
                out_ref[place(y, at_ref[2]), j] = back[y]


def add_core_kernel(keep_ref, other_ref, stay_ref, go_ref):
    total = keep_ref[...] + other_ref[...].astype(F32)
    stay_ref[...] = total[:2]
    go_ref[...] = total[2:].astype(BF16)


def add_y_kernel(keep_ref, other_ref, stay_ref, go_ref):
    stay_ref[...] = keep_ref[0] + other_ref[0].astype(F32)
    go_ref[...] = (keep_ref[1] + other_ref[1].astype(F32)).astype(BF16)


def add_last_kernel(keep_ref, other_ref, *refs):
    total = (keep_ref[...] + other_ref[...].astype(F32)).astype(BF16)
    for j in range(4):
        refs[j][...] = total[j]


def join_kernel(at_ref, *refs):
    for ref, step in zip(refs[:4], (0, 3, 1, 2)):
        refs[4][:, lax.rem(at_ref[1] + step, 4)] = ref[...].reshape(4, 16, 256)


def local(attention, residual, out_weight, norm_gain, grad_normed, grad_resid):
    x, y, c = (lax.axis_index(n).astype(jnp.int32) for n in ("x", "y", "c"))
    at = jnp.stack([c, x, y])
    swap = [(0, 1), (1, 0)]

    own = a2a(pieces(at, attention, out_weight), ("y", "x")).reshape(4, 4, 192, 256)
    own, weight = call(split_kernel, (shape((4, 4, 64, 256)), shape((1024, 512))), own)
    other = lax.ppermute(own, "c", swap)

    parts = call(forward_kernel, shape((32, 16, 512)), at, own, other, weight)
    parts = a2a(parts, ("zl", "c", "y"))

    normed, stream_out, stream_grad, cols = pl.pallas_call(
        norm_kernel,
        out_shape=(shape((16, 4096)),) * 3 + (shape((32, 96, 128)),),
        in_specs=[WHOLE] * 5,
        scratch_shapes=[pltpu.VMEM((16, 4096), F32)],
        compiler_params=PARAMS,
    )(parts, residual, norm_gain.reshape(1, 4096), grad_normed, grad_resid)

    grads, gain = call(
        unpack_kernel, (shape((512, 512)), shape((32, 128), F32)), a2a(cols, ("zl", "c", "y"))
    )

    blocks = call(weight_kernel, shape((4, 1088, 128)), at, own, other, grads, gain)
    blocks, weight = lax.optimization_barrier((blocks, weight))
    by_zh = call(weight_x_kernel, shape((4, 288, 128)), a2a(blocks, "x"))

    send, keep = call(
        back_kernel,
        (shape((4, 4, 64, 256)), shape((4, 4, 64, 256), F32)),
        at,
        grads,
        weight,
    )
    half = (2, 4, 64, 256)
    stay, go = call(
        add_core_kernel, (shape(half, F32), shape(half)), keep, lax.ppermute(send, "c", swap)
    )
    near = lax.ppermute(go, "y", apart(1))
    by_zh, near = lax.optimization_barrier((by_zh, near))
    parts = a2a(by_zh, "zh")
    stay, go = call(add_y_kernel, (shape(half[1:], F32), shape(half[1:])), stay, near)
    far = lax.ppermute(go, "y", apart(2))
    back = call(add_last_kernel, (shape((64, 256)),) * 4, stay, far)
    moved = [lax.ppermute(back[k], "x", ring(k)) for k in (1, 3, 2)]
    parts, moved[2] = lax.optimization_barrier((parts, moved[2]))
    weight_grad, gain = call(
        weight_zh_kernel, (shape((256, 128), F32), shape((32, 128), F32)), parts
    )
    attn_grad = call(join_kernel, shape((4, 4, 16, 256)), at, back[0], *moved).reshape(256, 256)
    return (normed, stream_out, stream_grad, attn_grad, weight_grad, gain.reshape(4096))


def solution(mesh):
    fine = Mesh(mesh.devices.reshape(4, 4, 2, 4, 4), AXES)
    dp, tensor = ("zh", "y", "c"), ("zl", "x")
    rows = P(dp + tensor, None)
    return jax.shard_map(
        local,
        mesh=fine,
        in_specs=(P(dp, tensor), rows, P(tensor, None), P(), rows, rows),
        out_specs=(rows, rows, rows, P(dp, tensor), P(tensor, dp), P()),
        check_vma=False,
    )
```

```python
import jax
import jax.numpy as jnp
from jax import lax
from jax.experimental import pallas as pl
from jax.experimental.pallas import tpu as pltpu
from jax.sharding import Mesh, PartitionSpec as P

BF16, F32 = jnp.bfloat16, jnp.float32
AXES = ("zh", "y", "c", "zl", "x")
PARAMS = pltpu.CompilerParams(vmem_limit_bytes=48 * 2**20)
SCALAR = pl.BlockSpec(memory_space=pltpu.SMEM)
WHOLE = pl.BlockSpec(memory_space=pltpu.VMEM)


def shape(dims, dtype=BF16):
    return jax.ShapeDtypeStruct(dims, dtype)


def call(kernel, out_shape, *args):
    specs = [SCALAR if a.dtype == jnp.int32 else WHOLE for a in args]
    return pl.pallas_call(kernel, out_shape=out_shape, in_specs=specs, compiler_params=PARAMS)(*args)


def a2a(value, axes):
    return lax.all_to_all(value, axes, 0, 0, tiled=True)


def ring(step):
    return [(i, (i + step) % 4) for i in range(4)]


def pieces_kernel(att_hbm_ref, weight_ref, out_ref, att_ref, quarter, rows, cols, sems):
    y, c = lax.axis_index("y"), lax.axis_index("c")
    first = pltpu.make_async_copy(att_hbm_ref, att_ref, sems.at[0])
    copy = pltpu.make_async_copy(
        weight_ref.at[pl.ds(pl.multiple_of(y * 64, 64), 64)], quarter, sems.at[1]
    )
    first.start()
    copy.start()
    first.wait()
    for x in range(4):
        for z in range(4):
            rows[x, z * 16 : z * 16 + 16] = att_ref[z * 64 + x * 16 : z * 64 + x * 16 + 16]
    copies = [
        pltpu.make_async_copy(rows, out_ref.at[y * 4 : y * 4 + 4, :64], sems.at[2 + y])
        for y in range(4)
    ]
    for one in copies:
        one.start()
    copy.wait()
    for there in range(4):
        for h in range(4):
            start = pl.multiple_of((h * 8 + there * 2 + c) * 128, 128)
            at, to = h // 2 * 64, h % 2 * 128
            cols[there, at : at + 64, to : to + 128] = quarter[:, pl.ds(start, 128)]
        for x in range(4):
            to_ref = out_ref.at[there * 4 + x, 64:]
            copies.append(pltpu.make_async_copy(cols.at[there], to_ref, sems.at[6 + there * 4 + x]))
            copies[-1].start()
    for one in copies:
        one.wait()


def pieces(attention, weight):
    return pl.pallas_call(
        pieces_kernel,
        out_shape=shape((16, 192, 256)),
        in_specs=[pl.BlockSpec(memory_space=pl.ANY)] * 2,
        out_specs=pl.BlockSpec(memory_space=pl.ANY),
        scratch_shapes=[
            pltpu.VMEM((256, 256), BF16),
            pltpu.VMEM((64, 4096), BF16),
            pltpu.VMEM((4, 64, 256), BF16),
            pltpu.VMEM((4, 128, 256), BF16),
            pltpu.SemaphoreType.DMA((22,)),
        ],
    )(attention, weight)


def split_kernel(parts_ref, att_ref, weight_ref):
    att_ref[...] = parts_ref[:, :, :64]
    for x in range(4):
        for half in range(2):
            weight_ref[x * 256 : x * 256 + 256, half * 256 : half * 256 + 256] = parts_ref[
                :, x, 64 + half * 64 : 128 + half * 64
            ].reshape(256, 256)


def apart(bits):
    return [(i, i ^ bits) for i in range(4)]


def forward_kernel(c_ref, own_ref, other_ref, weight_ref, out_ref):
    c = c_ref[0]
    for att_ref, core in ((own_ref, c), (other_ref, 1 - c)):
        total = jnp.zeros((256, 512), F32)
        for x in range(4):
            total += jnp.dot(
                att_ref[:, x].reshape(256, 256),
                weight_ref[x * 256 : x * 256 + 256],
                preferred_element_type=F32,
            )
        total = total.astype(BF16)
        for y in range(4):
            for z in range(4):
                at = (y * 4 + z) * 16
                out_ref[z * 8 + core * 4 + y] = total[at : at + 16]


def norm_kernel(
    parts_ref, residual_ref, gain_ref, upstream_ref, resid_grad_ref,
    normed_ref, stream_ref, grad_ref, cols_ref, projected_ref,
):
    for c in range(2):
        for y in range(4):
            at = c * 4 + y
            total = parts_ref[at].astype(F32)
            for k in range(1, 4):
                total += parts_ref[at + k * 8].astype(F32)
            for h in range(4):
                start = (h * 8 + y * 2 + c) * 128
                projected_ref[:, start : start + 128] = total[:, h * 128 : h * 128 + 128]
    projected = projected_ref[...]
    stream_out = (residual_ref[...].astype(F32) + projected).astype(BF16)
    stream_ref[...] = stream_out
    values = stream_out.astype(F32)
    inv_rms = lax.rsqrt(jnp.mean(values * values, axis=-1, keepdims=True) + 1e-05)
    unit_rows = values * inv_rms
    gain = gain_ref[...]
    normed_ref[...] = (unit_rows * gain).astype(BF16)
    upstream = upstream_ref[...].astype(F32)
    gain_grad = jnp.sum(upstream * unit_rows, axis=0, keepdims=True)
    scaled = upstream * gain
    inner = jnp.mean(scaled * unit_rows, axis=-1, keepdims=True)
    grad = (resid_grad_ref[...].astype(F32) + inv_rms * (scaled - unit_rows * inner)).astype(BF16)
    grad_ref[...] = grad
    for k in range(32):
        rows = gain_grad[:, k * 128 : k * 128 + 128].astype(BF16)
        rows = jnp.broadcast_to(rows[None], (4, 1, 128))
        for z in range(4):
            to = (z * 2 + k % 2) * 4
            cols_ref[to : to + 4, 64 + k // 2 : 65 + k // 2] = rows
    for c in range(2):
        for y in range(4):
            for h in range(4):
                start = (h * 8 + y * 2 + c) * 128
                for z in range(4):
                    to = (z * 2 + c) * 4 + y
                    cols_ref[to, h * 16 : h * 16 + 16] = grad[:, start : start + 128]


def unpack_kernel(parts_ref, grads_ref, gain_ref):
    gain_ref[...] = jnp.sum(parts_ref[:, 64:].astype(F32), axis=0)
    for k in range(32):
        at = (k % 8 * 4 + k // 8) * 16
        for h in range(4):
            grads_ref[at : at + 16, h * 128 : h * 128 + 128] = parts_ref[k, h * 16 : h * 16 + 16]


def weight_kernel(at_ref, own_ref, other_ref, grads_ref, gain_ref, out_ref):
    c = at_ref[0]
    gain = gain_ref[...]
    upper = gain.astype(BF16)
    lower = (gain - upper.astype(F32)).astype(BF16)
    for x in range(4):
        total = jnp.zeros((256, 512), F32)
        for att_ref, core in ((own_ref, c), (other_ref, 1 - c)):
            total += lax.dot_general(
                att_ref[:, x].reshape(256, 256),
                grads_ref[pl.ds(pl.multiple_of(core * 256, 256), 256)],
                (((0,), (0,)), ((), ())),
                preferred_element_type=F32,
            )
        total = total.astype(BF16)
        for h in range(4):
            out_ref[x, h * 256 : h * 256 + 256] = total[:, h * 128 : h * 128 + 128]
        out_ref[x, 1024:1040] = upper
        out_ref[x, 1040:] = lower


def weight_x_kernel(parts_ref, out_ref):
    total = parts_ref[0].astype(F32)
    for k in range(1, 4):
        total += parts_ref[k].astype(F32)
    for h in range(4):
        out_ref[h, :256] = total[h * 256 : h * 256 + 256].astype(BF16)
        out_ref[h, 256:] = (total[1024:1040] + total[1040:]).astype(BF16)


def weight_zh_kernel(parts_ref, weight_ref, gain_ref):
    total = parts_ref[0].astype(F32)
    for k in range(1, 4):
        total += parts_ref[k].astype(F32)
    weight_ref[...] = total[:256]
    gain_ref[...] = total[256:]


def place(there, here):
    apart = there ^ here
    return (apart & 1) * 2 + (apart >> 1)


def back_kernel(at_ref, grads_ref, weight_ref, send_ref, keep_ref):
    for out_ref, core in ((send_ref, 1 - at_ref[0]), (keep_ref, at_ref[0])):
        rows = grads_ref[pl.ds(pl.multiple_of(core * 256, 256), 256)]
        for j in range(4):
            start = pl.multiple_of(lax.rem(at_ref[1] + j, 4) * 256, 256)
            back = lax.dot_general(
                rows,
                weight_ref[pl.ds(start, 256)],
                (((1,), (1,)), ((), ())),
                preferred_element_type=F32,
            )
            back = back.reshape(4, 64, 256).astype(out_ref.dtype)
            for y in range(4):
                out_ref[place(y, at_ref[2]), j] = back[y]


def add_core_kernel(keep_ref, other_ref, stay_ref, go_ref):
    total = keep_ref[...] + other_ref[...].astype(F32)
    stay_ref[...] = total[:2]
    go_ref[...] = total[2:].astype(BF16)


def add_y_kernel(keep_ref, other_ref, stay_ref, go_ref):
    stay_ref[...] = keep_ref[0] + other_ref[0].astype(F32)
    go_ref[...] = (keep_ref[1] + other_ref[1].astype(F32)).astype(BF16)


def add_last_kernel(keep_ref, other_ref, *refs):
    total = (keep_ref[...] + other_ref[...].astype(F32)).astype(BF16)
    for j in range(4):
        refs[j][...] = total[j]


def join_kernel(at_ref, gain_ref, other_ref, *refs):
    ours, gain, other = at_ref[0] == 0, gain_ref[...], other_ref[...]
    first, last = jnp.where(ours, gain, other), jnp.where(ours, other, gain)
    for k in range(16):
        refs[5][2 * k : 2 * k + 1] = first[k : k + 1]
        refs[5][2 * k + 1 : 2 * k + 2] = last[k : k + 1]
    for ref, step in zip(refs[:4], (0, 3, 1, 2)):
        refs[4][:, lax.rem(at_ref[1] + step, 4)] = ref[...].reshape(4, 16, 256)


def local(attention, residual, out_weight, norm_gain, grad_normed, grad_resid):
    x, y, c = (lax.axis_index(n).astype(jnp.int32) for n in ("x", "y", "c"))
    at = jnp.stack([c, x, y])
    swap = [(0, 1), (1, 0)]

    own = a2a(pieces(attention, out_weight), ("y", "x")).reshape(4, 4, 192, 256)
    own, weight = call(split_kernel, (shape((4, 4, 64, 256)), shape((1024, 512))), own)
    other = lax.ppermute(own, "c", swap)

    parts = call(forward_kernel, shape((32, 16, 512)), at, own, other, weight)
    parts = a2a(parts, ("zl", "c", "y"))

    normed, stream_out, stream_grad, cols = pl.pallas_call(
        norm_kernel,
        out_shape=(shape((16, 4096)),) * 3 + (shape((32, 80, 128)),),
        in_specs=[WHOLE] * 5,
        scratch_shapes=[pltpu.VMEM((16, 4096), F32)],
        compiler_params=PARAMS,
    )(parts, residual, norm_gain.reshape(1, 4096), grad_normed, grad_resid)

    grads, gain = call(
        unpack_kernel, (shape((512, 512)), shape((16, 128), F32)), a2a(cols, ("zl", "c", "y"))
    )

    blocks = call(weight_kernel, shape((4, 1056, 128)), at, own, other, grads, gain)
    blocks, weight = lax.optimization_barrier((blocks, weight))
    by_zh = call(weight_x_kernel, shape((4, 272, 128)), a2a(blocks, "x"))

    send, keep = call(
        back_kernel,
        (shape((4, 4, 64, 256)), shape((4, 4, 64, 256), F32)),
        at,
        grads,
        weight,
    )
    half = (2, 4, 64, 256)
    stay, go = call(
        add_core_kernel, (shape(half, F32), shape(half)), keep, lax.ppermute(send, "c", swap)
    )
    near = lax.ppermute(go, "y", apart(1))
    by_zh, near = lax.optimization_barrier((by_zh, near))
    parts = a2a(by_zh, "zh")
    stay, go = call(add_y_kernel, (shape(half[1:], F32), shape(half[1:])), stay, near)
    far = lax.ppermute(go, "y", apart(2))
    back = call(add_last_kernel, (shape((64, 256)),) * 4, stay, far)
    moved = [lax.ppermute(back[k], "x", ring(k)) for k in (1, 3, 2)]
    parts, moved[2] = lax.optimization_barrier((parts, moved[2]))
    weight_grad, gain = call(
        weight_zh_kernel, (shape((256, 128), F32), shape((16, 128), F32)), parts
    )
    attn_grad, gain_grad = call(
        join_kernel,
        (shape((4, 4, 16, 256)), shape((32, 128), F32)),
        at,
        gain,
        lax.ppermute(gain, "c", swap),
        back[0],
        *moved,
    )
    attn_grad, gain_grad = attn_grad.reshape(256, 256), gain_grad.reshape(4096)
    return (normed, stream_out, stream_grad, attn_grad, weight_grad, gain_grad)


def solution(mesh):
    fine = Mesh(mesh.devices.reshape(4, 4, 2, 4, 4), AXES)
    dp, tensor = ("zh", "y", "c"), ("zl", "x")
    rows = P(dp + tensor, None)
    return jax.shard_map(
        local,
        mesh=fine,
        in_specs=(P(dp, tensor), rows, P(tensor, None), P(), rows, rows),
        out_specs=(rows, rows, rows, P(dp, tensor), P(tensor, dp), P()),
        check_vma=False,
    )
```

```python
import jax
import jax.numpy as jnp
from jax import lax
from jax.experimental import pallas as pl
from jax.experimental.pallas import tpu as pltpu
from jax.sharding import Mesh, PartitionSpec as P

BF16, F32 = jnp.bfloat16, jnp.float32
AXES = ("zh", "y", "c", "zl", "x")
PARAMS = pltpu.CompilerParams(vmem_limit_bytes=48 * 2**20)
SCALAR = pl.BlockSpec(memory_space=pltpu.SMEM)
WHOLE = pl.BlockSpec(memory_space=pltpu.VMEM)


def shape(dims, dtype=BF16):
    return jax.ShapeDtypeStruct(dims, dtype)


def call(kernel, out_shape, *args):
    specs = [SCALAR if a.dtype == jnp.int32 else WHOLE for a in args]
    return pl.pallas_call(kernel, out_shape=out_shape, in_specs=specs, compiler_params=PARAMS)(*args)


def a2a(value, axes):
    return lax.all_to_all(value, axes, 0, 0, tiled=True)


def ring(step):
    return [(i, (i + step) % 4) for i in range(4)]


def pieces_kernel(att_hbm_ref, weight_ref, out_ref, att_ref, quarter, rows, cols, sems):
    y, c = lax.axis_index("y"), lax.axis_index("c")
    first = pltpu.make_async_copy(att_hbm_ref, att_ref, sems.at[0])
    copy = pltpu.make_async_copy(
        weight_ref.at[pl.ds(pl.multiple_of(y * 64, 64), 64)], quarter, sems.at[1]
    )
    first.start()
    copy.start()
    first.wait()
    for x in range(4):
        for z in range(4):
            rows[x, z * 16 : z * 16 + 16] = att_ref[z * 64 + x * 16 : z * 64 + x * 16 + 16]
    copies = [
        pltpu.make_async_copy(rows, out_ref.at[y * 4 : y * 4 + 4, :64], sems.at[2 + y])
        for y in range(4)
    ]
    for one in copies:
        one.start()
    copy.wait()
    for there in range(4):
        for h in range(4):
            start = pl.multiple_of((h * 8 + there * 2 + c) * 128, 128)
            at, to = h // 2 * 64, h % 2 * 128
            cols[there, at : at + 64, to : to + 128] = quarter[:, pl.ds(start, 128)]
        for x in range(4):
            to_ref = out_ref.at[there * 4 + x, 64:]
            copies.append(pltpu.make_async_copy(cols.at[there], to_ref, sems.at[6 + there * 4 + x]))
            copies[-1].start()
    for one in copies:
        one.wait()


def pieces(attention, weight):
    return pl.pallas_call(
        pieces_kernel,
        out_shape=shape((16, 192, 256)),
        in_specs=[pl.BlockSpec(memory_space=pl.ANY)] * 2,
        out_specs=pl.BlockSpec(memory_space=pl.ANY),
        scratch_shapes=[
            pltpu.VMEM((256, 256), BF16),
            pltpu.VMEM((64, 4096), BF16),
            pltpu.VMEM((4, 64, 256), BF16),
            pltpu.VMEM((4, 128, 256), BF16),
            pltpu.SemaphoreType.DMA((22,)),
        ],
    )(attention, weight)


def split_kernel(parts_ref, att_ref, weight_ref):
    att_ref[...] = parts_ref[:, :, :64]
    for x in range(4):
        for half in range(2):
            weight_ref[x * 256 : x * 256 + 256, half * 256 : half * 256 + 256] = parts_ref[
                :, x, 64 + half * 64 : 128 + half * 64
            ].reshape(256, 256)


def apart(bits):
    return [(i, i ^ bits) for i in range(4)]


def forward_kernel(c_ref, own_ref, other_ref, weight_ref, out_ref):
    c = c_ref[0]
    for att_ref, core in ((own_ref, c), (other_ref, 1 - c)):
        total = jnp.zeros((256, 512), F32)
        for x in range(4):
            total += jnp.dot(
                att_ref[:, x].reshape(256, 256),
                weight_ref[x * 256 : x * 256 + 256],
                preferred_element_type=F32,
            )
        total = total.astype(BF16)
        for y in range(4):
            for z in range(4):
                at = (y * 4 + z) * 16
                out_ref[z * 8 + core * 4 + y] = total[at : at + 16]


def norm_kernel(
    parts_ref, residual_ref, gain_ref, upstream_ref, resid_grad_ref,
    normed_ref, stream_ref, grad_ref, cols_ref, projected_ref, rows_ref,
):
    for c in range(2):
        for y in range(4):
            at = c * 4 + y
            total = parts_ref[at].astype(F32)
            for k in range(1, 4):
                total += parts_ref[at + k * 8].astype(F32)
            for h in range(4):
                start = (h * 8 + y * 2 + c) * 128
                projected_ref[:, start : start + 128] = total[:, h * 128 : h * 128 + 128]
    projected = projected_ref[...]
    stream_out = (residual_ref[...].astype(F32) + projected).astype(BF16)
    stream_ref[...] = stream_out
    values = stream_out.astype(F32)
    inv_rms = lax.rsqrt(jnp.mean(values * values, axis=-1, keepdims=True) + 1e-05)
    unit_rows = values * inv_rms
    gain = gain_ref[...]
    normed_ref[...] = (unit_rows * gain).astype(BF16)
    upstream = upstream_ref[...].astype(F32)
    gain_grad = jnp.sum(upstream * unit_rows, axis=0, keepdims=True)
    scaled = upstream * gain
    inner = jnp.mean(scaled * unit_rows, axis=-1, keepdims=True)
    grad = (resid_grad_ref[...].astype(F32) + inv_rms * (scaled - unit_rows * inner)).astype(BF16)
    grad_ref[...] = grad
    for k in range(32):
        at = k % 2 * 16 + k // 2
        rows_ref[at : at + 1] = gain_grad[:, k * 128 : k * 128 + 128]
    for to in range(32):
        at = to // 4 % 2 * 16
        cols_ref[to, 64:] = rows_ref[at : at + 16].astype(BF16)
    for c in range(2):
        for y in range(4):
            for h in range(4):
                start = (h * 8 + y * 2 + c) * 128
                for z in range(4):
                    to = (z * 2 + c) * 4 + y
                    cols_ref[to, h * 16 : h * 16 + 16] = grad[:, start : start + 128]


def unpack_kernel(parts_ref, grads_ref, gain_ref):
    gain_ref[...] = jnp.sum(parts_ref[:, 64:].astype(F32), axis=0)
    for k in range(32):
        at = (k % 8 * 4 + k // 8) * 16
        for h in range(4):
            grads_ref[at : at + 16, h * 128 : h * 128 + 128] = parts_ref[k, h * 16 : h * 16 + 16]


def weight_kernel(at_ref, own_ref, other_ref, grads_ref, gain_ref, out_ref):
    c = at_ref[0]
    gain = gain_ref[...]
    upper = gain.astype(BF16)
    lower = (gain - upper.astype(F32)).astype(BF16)
    total = jnp.zeros((256, 512), F32)
    for att_ref, core in ((own_ref, c), (other_ref, 1 - c)):
        total += lax.dot_general(
            att_ref[:, pl.program_id(0)].reshape(256, 256),
            grads_ref[pl.ds(pl.multiple_of(core * 256, 256), 256)],
            (((0,), (0,)), ((), ())),
            preferred_element_type=F32,
        )
    total = total.astype(BF16)
    for h in range(4):
        out_ref[0, h * 256 : h * 256 + 256] = total[:, h * 128 : h * 128 + 128]
    out_ref[0, 1024:1040] = upper
    out_ref[0, 1040:] = lower


def weight_x_kernel(parts_ref, out_ref):
    total = parts_ref[0].astype(F32)
    for k in range(1, 4):
        total += parts_ref[k].astype(F32)
    for h in range(4):
        out_ref[h, :256] = total[h * 256 : h * 256 + 256].astype(BF16)
        out_ref[h, 256:] = (total[1024:1040] + total[1040:]).astype(BF16)


def weight_zh_kernel(parts_ref, weight_ref):
    total = parts_ref[0, :256].astype(F32)
    for k in range(1, 4):
        total += parts_ref[k, :256].astype(F32)
    weight_ref[...] = total


def gain_zh_kernel(parts_ref, gain_ref):
    gain_ref[...] = jnp.sum(parts_ref[:, 256:].astype(F32), axis=0)


def place(there, here):
    apart = there ^ here
    return (apart & 1) * 2 + (apart >> 1)


def back_kernel(at_ref, grads_ref, weight_ref, send_ref, keep_ref):
    for out_ref, core in ((send_ref, 1 - at_ref[0]), (keep_ref, at_ref[0])):
        rows = grads_ref[pl.ds(pl.multiple_of(core * 256, 256), 256)]
        for j in range(4):
            start = pl.multiple_of(lax.rem(at_ref[1] + j, 4) * 256, 256)
            back = lax.dot_general(
                rows,
                weight_ref[pl.ds(start, 256)],
                (((1,), (1,)), ((), ())),
                preferred_element_type=F32,
            )
            back = back.reshape(4, 64, 256).astype(out_ref.dtype)
            for y in range(4):
                out_ref[place(y, at_ref[2]), j] = back[y]


def add_core_kernel(keep_ref, other_ref, stay_ref, go_ref):
    total = keep_ref[...] + other_ref[...].astype(F32)
    stay_ref[...] = total[:2]
    go_ref[...] = total[2:].astype(BF16)


def add_y_kernel(keep_ref, other_ref, stay_ref, go_ref):
    stay_ref[...] = keep_ref[0] + other_ref[0].astype(F32)
    go_ref[...] = (keep_ref[1] + other_ref[1].astype(F32)).astype(BF16)


def add_last_kernel(keep_ref, other_ref, *refs):
    total = (keep_ref[...] + other_ref[...].astype(F32)).astype(BF16)
    for j in range(4):
        refs[j][...] = total[j]


def join_kernel(at_ref, gain_ref, other_ref, *refs):
    ours, gain, other = at_ref[0] == 0, gain_ref[...], other_ref[...]
    first, last = jnp.where(ours, gain, other), jnp.where(ours, other, gain)
    for k in range(16):
        refs[5][2 * k : 2 * k + 1] = first[k : k + 1]
        refs[5][2 * k + 1 : 2 * k + 2] = last[k : k + 1]
    for ref, step in zip(refs[:4], (0, 3, 1, 2)):
        refs[4][:, lax.rem(at_ref[1] + step, 4)] = ref[...].reshape(4, 16, 256)


def local(attention, residual, out_weight, norm_gain, grad_normed, grad_resid):
    x, y, c = (lax.axis_index(n).astype(jnp.int32) for n in ("x", "y", "c"))
    at = jnp.stack([c, x, y])
    swap = [(0, 1), (1, 0)]

    own = a2a(pieces(attention, out_weight), ("y", "x")).reshape(4, 4, 192, 256)
    own, weight = call(split_kernel, (shape((4, 4, 64, 256)), shape((1024, 512))), own)
    other = lax.ppermute(own, "c", swap)

    parts = call(forward_kernel, shape((32, 16, 512)), at, own, other, weight)
    parts = a2a(parts, ("zl", "c", "y"))

    normed, stream_out, stream_grad, cols = pl.pallas_call(
        norm_kernel,
        out_shape=(shape((16, 4096)),) * 3 + (shape((32, 80, 128)),),
        in_specs=[WHOLE] * 5,
        scratch_shapes=[pltpu.VMEM((16, 4096), F32), pltpu.VMEM((32, 128), F32)],
        compiler_params=PARAMS,
    )(parts, residual, norm_gain.reshape(1, 4096), grad_normed, grad_resid)

    grads, gain = call(
        unpack_kernel, (shape((512, 512)), shape((16, 128), F32)), a2a(cols, ("zl", "c", "y"))
    )

    blocks = pl.pallas_call(
        weight_kernel,
        grid=(4,),
        out_shape=shape((4, 1056, 128)),
        in_specs=[SCALAR] + [WHOLE] * 4,
        out_specs=pl.BlockSpec((1, 1056, 128), lambda x: (x, 0, 0)),
        compiler_params=PARAMS,
    )(at, own, other, grads, gain)
    blocks, weight = lax.optimization_barrier((blocks, weight))
    by_zh = call(weight_x_kernel, shape((4, 272, 128)), a2a(blocks, "x"))

    send, keep = call(
        back_kernel,
        (shape((4, 4, 64, 256)), shape((4, 4, 64, 256), F32)),
        at,
        grads,
        weight,
    )
    half = (2, 4, 64, 256)
    stay, go = call(
        add_core_kernel, (shape(half, F32), shape(half)), keep, lax.ppermute(send, "c", swap)
    )
    near = lax.ppermute(go, "y", apart(1))
    by_zh, near = lax.optimization_barrier((by_zh, near))
    parts = a2a(by_zh, "zh")
    stay, go = call(add_y_kernel, (shape(half[1:], F32), shape(half[1:])), stay, near)
    far = lax.ppermute(go, "y", apart(2))
    back = call(add_last_kernel, (shape((64, 256)),) * 4, stay, far)
    moved = [lax.ppermute(back[k], "x", ring(k)) for k in (1, 3, 2)]
    parts, moved[2] = lax.optimization_barrier((parts, moved[2]))
    gain = call(gain_zh_kernel, shape((16, 128), F32), parts)
    weight_grad = call(weight_zh_kernel, shape((256, 128), F32), parts)
    attn_grad, gain_grad = call(
        join_kernel,
        (shape((4, 4, 16, 256)), shape((32, 128), F32)),
        at,
        gain,
        lax.ppermute(gain, "c", swap),
        back[0],
        *moved,
    )
    attn_grad, gain_grad = attn_grad.reshape(256, 256), gain_grad.reshape(4096)
    return (normed, stream_out, stream_grad, attn_grad, weight_grad, gain_grad)


def solution(mesh):
    fine = Mesh(mesh.devices.reshape(4, 4, 2, 4, 4), AXES)
    dp, tensor = ("zh", "y", "c"), ("zl", "x")
    rows = P(dp + tensor, None)
    return jax.shard_map(
        local,
        mesh=fine,
        in_specs=(P(dp, tensor), rows, P(tensor, None), P(), rows, rows),
        out_specs=(rows, rows, rows, P(dp, tensor), P(tensor, dp), P()),
        check_vma=False,
    )
```
